512 devices in a mesh: inst: 32 (over x_hi, z), tp: 16 (over x_lo, y, core).
Axes of the slice: x: 4 (x_hi: 2, x_lo: 2; x = x_hi * 2 + x_lo), y: 4, z: 16, core: 2. Of those that a mesh axis runs over, the one named last changes fastest.
Arguments:
- kv_pool: bfloat16 [1792, 16, 2, 128, 128], P('inst', 'tp'), may hold values from -4 to 4, as said below
- block_table: int32 [192, 8], P('inst'), may hold values from 0 to 55, as said below
- mig_table: int32 [32, 8], P('inst'), may hold values from 0 to 55, as said below
- query_stay: bfloat16 [192, 8192], P('inst', 'tp'), may hold values from -8 to 8
- query_mig: bfloat16 [32, 8192], P('inst', 'tp'), may hold values from -8 to 8
- new_stay: bfloat16 [192, 16, 2, 128], P('inst', 'tp'), may hold values from -4 to 4, as said below
- new_mig: bfloat16 [32, 16, 2, 128], P('inst', 'tp'), may hold values from -4 to 4, as said below
- len_stay: int32 [192], P('inst'), may hold values from 1 to 1024, as said below
- len_mig: int32 [32], P('inst'), may hold values from 1 to 1024, as said below
- hidden_stay: bfloat16 [192, 8192], P('inst', 'tp'), may hold values from -60 to 60
- hidden_mig: bfloat16 [32, 8192], P('inst', 'tp'), may hold values from -60 to 60
- norm_gain: bfloat16 [8192], P('tp'), may hold values from 0.099609375 to 1.8984375
- partner_mask: int32 [1], replicated, may hold values from 1 to 31
Outputs:
- attended: bfloat16 [224, 8192], P('inst', 'tp')
- arrived_pages: bfloat16 [32, 8, 16, 2, 128, 128], P('inst', None, 'tp')
- normed: bfloat16 [224, 8192], P('inst', 'tp')
The draws below stay inside these ranges and needn't reach their ends.
Inputs may be any that keep to these rules, and one draw needn't show every extreme that they name: Each instance's block_table and mig_table rows together name each of its 56 local pages exactly once. `mig_table`: local page numbers, as in block_table. `len_stay`: lengths count cached tokens with the new one. `len_mig`: lengths count cached tokens with the new one. `kv_pool`: slot s holds kv head s // 2; slots of one head are equal. `new_stay`: slots of one kv head are equal. `new_mig`: slots of one kv head are equal. Instance i is matched with instance i XOR partner_mask[0].
All inputs are finite; a program needn't handle non-finite values.
Results may differ from the reference program's by a relative error of at most 0.0047.
Values may be sent and summed in bfloat16 or wider, within the bound.
A program may use at most 64 MiB of HBM per device.

```python
import math
import jax
import jax.numpy as jnp
from jax import lax

D = 8192
HEADS = 64
KV_HEADS = 8
HD = 128
PAGE = 128
PAGES_REQ = 8
REQ = 6
MIG = 1
INSTANCES = 32
SLOTS = 16
POOL = 56
MAXLEN = 1024
N_INST = 32


def copy_heads(values):
    return jnp.repeat(values.astype(jnp.bfloat16), SLOTS // KV_HEADS, axis=1)


def draw_kv_pool(key, part):
    key = jax.random.fold_in(key, 1)
    shape = (INSTANCES * POOL, KV_HEADS, 2, PAGE, HD)
    values = jnp.clip(jax.random.normal(key, shape, jnp.float32), -4.0, 4.0)
    return copy_heads(values)


def drawn_queries(key, row_count):
    values = jnp.clip(jax.random.normal(key, (row_count, HEADS * HD), jnp.float32), -4.0, 4.0)
    return values.astype(jnp.bfloat16)


def draw_query_stay(key, part):
    key = jax.random.fold_in(key, 2)
    return drawn_queries(key, INSTANCES * REQ)


def draw_query_mig(key, part):
    key = jax.random.fold_in(key, 3)
    return drawn_queries(key, INSTANCES * MIG)


def draw_new_stay(key, part):
    key = jax.random.fold_in(key, 4)
    values = jnp.clip(jax.random.normal(key, (INSTANCES * REQ, KV_HEADS, 2, HD), jnp.float32), -4.0, 4.0)
    return copy_heads(values)


def draw_new_mig(key, part):
    key = jax.random.fold_in(key, 5)
    values = jnp.clip(jax.random.normal(key, (INSTANCES * MIG, KV_HEADS, 2, HD), jnp.float32), -4.0, 4.0)
    return copy_heads(values)


def scaled_rows(key, values):
    row_count = values.shape[0]
    row_scale = jnp.exp(jax.random.uniform(jax.random.fold_in(key, 7), (row_count, 1), jnp.float32, 0.0, math.log(10.0)))
    column = lax.broadcasted_iota(jnp.int32, (1, D), 1).astype(jnp.float32)
    column_scale = jnp.exp(column * (math.log(3.0) / D))
    return (values * row_scale * column_scale).astype(jnp.bfloat16)


def draw_hidden_stay(key, part):
    key = jax.random.fold_in(key, 6)
    values = jnp.clip(jax.random.normal(key, (INSTANCES * REQ, D), jnp.float32), -2.0, 2.0)
    return scaled_rows(key, values)


def draw_hidden_mig(key, part):
    key = jax.random.fold_in(key, 9)
    values = jnp.clip(jax.random.normal(key, (INSTANCES * MIG, D), jnp.float32), -2.0, 2.0)
    return scaled_rows(key, values)


def ragged_lengths(key, per_group):
    ceiling = jax.random.randint(jax.random.fold_in(key, 1), (INSTANCES, 1), MAXLEN // 4, MAXLEN + 1)
    values = jax.random.randint(jax.random.fold_in(key, 2), (INSTANCES, per_group), 1, MAXLEN + 1)
    values = 1 + jnp.remainder(values - 1, ceiling)
    flat = values.reshape(-1)
    chosen = jax.random.randint(jax.random.fold_in(key, 3), (), 0, INSTANCES * per_group)
    return jnp.where(jnp.arange(INSTANCES * per_group) == chosen, MAXLEN, flat).astype(jnp.int32)


def draw_len_stay(key, part):
    key = jax.random.fold_in(key, 11)
    return ragged_lengths(key, REQ)


def draw_len_mig(key, part):
    key = jax.random.fold_in(key, 12)
    return ragged_lengths(key, MIG)


def pool_order(key):
    instance_keys = jax.random.split(jax.random.fold_in(key, 500), INSTANCES)
    return jax.vmap(lambda sub_key: jax.random.permutation(sub_key, POOL))(instance_keys)


def draw_block_table(key, part):
    order = pool_order(key)
    return order[:, :REQ * PAGES_REQ].reshape(INSTANCES * REQ, PAGES_REQ).astype(jnp.int32)


def draw_mig_table(key, part):
    order = pool_order(key)
    return order[:, REQ * PAGES_REQ:].reshape(INSTANCES * MIG, PAGES_REQ).astype(jnp.int32)


def setup_inputs(seed: int = 0) -> dict:
    arg_keys = jax.random.split(jax.random.key(seed), 14)
    kv_pool = draw_kv_pool(jax.random.fold_in(arg_keys[13], 71), 0)
    block_table = draw_block_table(jax.random.fold_in(arg_keys[13], 71), 0)
    mig_table = draw_mig_table(jax.random.fold_in(arg_keys[13], 71), 0)
    query_stay = draw_query_stay(jax.random.fold_in(arg_keys[13], 71), 0)
    query_mig = draw_query_mig(jax.random.fold_in(arg_keys[13], 71), 0)
    new_stay = draw_new_stay(jax.random.fold_in(arg_keys[13], 71), 0)
    new_mig = draw_new_mig(jax.random.fold_in(arg_keys[13], 71), 0)
    len_stay = draw_len_stay(jax.random.fold_in(arg_keys[13], 71), 0)
    len_mig = draw_len_mig(jax.random.fold_in(arg_keys[13], 71), 0)
    hidden_stay = draw_hidden_stay(jax.random.fold_in(arg_keys[13], 71), 0)
    hidden_mig = draw_hidden_mig(jax.random.fold_in(arg_keys[13], 71), 0)
    norm_gain = jnp.clip(1.0 + 0.18 * jax.random.normal(arg_keys[11], (D,), jnp.float32), 0.099609375, 1.8984375).astype(jnp.bfloat16)
    partner_mask = jax.random.randint(arg_keys[12], (1,), 1, N_INST).astype(jnp.int32)
    return {"kv_pool": kv_pool, "block_table": block_table, "mig_table": mig_table, "query_stay": query_stay, "query_mig": query_mig, "new_stay": new_stay, "new_mig": new_mig, "len_stay": len_stay, "len_mig": len_mig, "hidden_stay": hidden_stay, "hidden_mig": hidden_mig, "norm_gain": norm_gain, "partner_mask": partner_mask}


def write_token(pages, new_kv, length):
    page_count = pages.shape[0]
    page_size = pages.shape[3]
    shape = (page_count, 1, 1, page_size, 1)
    position = lax.broadcasted_iota(jnp.int32, shape, 0) * page_size + lax.broadcasted_iota(jnp.int32, shape, 3)
    return jnp.where(position == length - 1, new_kv[None, :, :, None, :], pages)

def attend_one(query, pages, length):
    page_count = pages.shape[0]
    slot_count = pages.shape[1]
    page_size = pages.shape[3]
    head_size = pages.shape[4]
    group_size = query.shape[0] // (slot_count * head_size)
    queries = query.reshape(slot_count, group_size, head_size).astype(jnp.float32)
    scores = jnp.einsum('sgd,pstd->sgpt', queries, pages[:, :, 0].astype(jnp.float32)) * head_size ** (-0.5)
    shape = (1, 1, page_count, page_size)
    position = lax.broadcasted_iota(jnp.int32, shape, 2) * page_size + lax.broadcasted_iota(jnp.int32, shape, 3)
    visible = position < length
    scores = jnp.where(visible, scores, -1e+30)
    highest = lax.optimization_barrier(jnp.max(scores, axis=(2, 3), keepdims=True))
    weights = jnp.where(visible, jnp.exp(scores - highest), 0.0)
    weights = weights / lax.optimization_barrier(jnp.sum(weights, axis=(2, 3), keepdims=True))
    rounded = lax.optimization_barrier(weights.astype(jnp.bfloat16)).astype(jnp.float32)
    mixed = jnp.einsum('sgpt,pstd->sgd', rounded, pages[:, :, 1].astype(jnp.float32))
    return mixed.reshape(-1).astype(jnp.bfloat16)

def pick(array, instance):
    return lax.dynamic_index_in_dim(array, instance, 0, keepdims=False)

def reference(kv_pool, block_table, mig_table, query_stay, query_mig, new_stay, new_mig, len_stay, len_mig, hidden_stay, hidden_mig, norm_gain, partner_mask):
    pools = kv_pool.reshape(INSTANCES, POOL, SLOTS, 2, PAGE, HD)
    stay_tables = block_table.reshape(INSTANCES, REQ, PAGES_REQ)
    leave_tables = mig_table.reshape(INSTANCES, MIG, PAGES_REQ)
    stay_queries = query_stay.reshape(INSTANCES, REQ, HEADS * HD)
    leave_queries = query_mig.reshape(INSTANCES, MIG, HEADS * HD)
    stay_new = new_stay.reshape(INSTANCES, REQ, SLOTS, 2, HD)
    leave_new = new_mig.reshape(INSTANCES, MIG, SLOTS, 2, HD)
    stay_len = len_stay.reshape(INSTANCES, REQ)
    leave_len = len_mig.reshape(INSTANCES, MIG)
    stay_rows = hidden_stay.reshape(INSTANCES, REQ, D)
    leave_rows = hidden_mig.reshape(INSTANCES, MIG, D)
    gain_f = norm_gain.astype(jnp.float32)

    def per_instance(instance):
        partner = jnp.bitwise_xor(instance, partner_mask[0])
        own_pool = pick(pools, instance)
        far_pool = pick(pools, partner)
        own_len = pick(stay_len, instance)
        far_len = pick(leave_len, partner)
        staying = jax.vmap(write_token)(own_pool[pick(stay_tables, instance)], pick(stay_new, instance), own_len)
        leaving = jax.vmap(write_token)(far_pool[pick(leave_tables, partner)], pick(leave_new, partner), far_len)
        mixed_stay = jax.vmap(attend_one)(pick(stay_queries, instance), staying, own_len)
        mixed_in = jax.vmap(attend_one)(pick(leave_queries, partner), leaving, far_len)
        residual = jnp.concatenate([pick(stay_rows, instance), pick(leave_rows, partner)], axis=0).astype(jnp.float32)
        mean_square = lax.optimization_barrier(jnp.sum(residual * residual, axis=1, keepdims=True)) / D
        normed_rows = (residual * lax.rsqrt(mean_square + 1e-05) * gain_f).astype(jnp.bfloat16)
        return (jnp.concatenate([mixed_stay, mixed_in], axis=0), leaving, normed_rows)
    attended, arrived, normed = lax.map(per_instance, jnp.arange(INSTANCES, dtype=jnp.int32))
    attended = attended.reshape(INSTANCES * (REQ + MIG), HEADS * HD)
    arrived = arrived.reshape(INSTANCES * MIG, PAGES_REQ, SLOTS, 2, PAGE, HD)
    normed = normed.reshape(INSTANCES * (REQ + MIG), D)
    return (attended, arrived, normed)
```

```python
import functools

import jax
import jax.numpy as jnp
from jax import lax
from jax.experimental import pallas as pl
from jax.experimental.pallas import tpu as pltpu
from jax.sharding import PartitionSpec as P

MESH = pl.DeviceIdType.MESH
D = 8192
LANES = 128
GROUP = 4
PARTS = 8


def flipped(index, mask):
    bit = 1
    total = index
    while bit <= mask:
        if mask & bit:
            total = total + bit - 2 * bit * ((index // bit) % 2)
        bit *= 2
    return total


def attend(pool, table, row, query, new_kv, length):
    pages = table.shape[1]
    page = pool.shape[2]
    new_key = new_kv[0:1].astype(jnp.float32)
    new_value = new_kv[1:2].astype(jnp.float32)
    scale = LANES ** (-0.5)
    new_score = jnp.sum(query.astype(jnp.float32) * new_key, axis=1, keepdims=True) * scale
    column = lax.broadcasted_iota(jnp.int32, (query.shape[0], page), 1)
    scores = []
    for j in range(pages):
        score = lax.dot_general(
            query,
            pool[table[row, j], 0],
            (((1,), (1,)), ((), ())),
            preferred_element_type=jnp.float32,
        )
        score = score * scale
        position = column + j * page
        score = jnp.where(position == length - 1, new_score, score)
        scores.append(jnp.where(position < length, score, -1e30))
    highest = functools.reduce(jnp.maximum, scores)
    highest = jnp.max(highest, axis=1, keepdims=True)
    weights = [
        jnp.where(column + j * page < length, jnp.exp(s - highest), 0.0)
        for j, s in enumerate(scores)
    ]
    total = jnp.sum(functools.reduce(jnp.add, weights), axis=1, keepdims=True)
    mixed = jnp.zeros((query.shape[0], LANES), jnp.float32)
    last = jnp.zeros((query.shape[0], page), jnp.float32)
    for j, w in enumerate(weights):
        w = (w / total).astype(jnp.bfloat16).astype(jnp.float32)
        is_last = column + j * page == length - 1
        last = last + jnp.where(is_last, w, 0.0)
        w = jnp.where(is_last, 0.0, w).astype(jnp.bfloat16)
        mixed = mixed + jnp.dot(w, pool[table[row, j], 1], preferred_element_type=jnp.float32)
    return mixed + jnp.sum(last, axis=1, keepdims=True) * new_value


def kernel(
    mask,
    tp_bits,
    kv_ref,
    block_table,
    mig_table,
    len_stay,
    len_mig,
    query_stay,
    query_mig,
    new_stay,
    new_mig,
    hidden_stay,
    hidden_mig,
    gain,
    attended,
    arrived,
    normed,
    pool,
    out_pages,
    queries,
    mixed,
    rows,
    sums_out,
    sums_in,
    note_out,
    note_in,
    pool_sem,
    page_send,
    page_recv,
    pass_send,
    pass_recv,
    sum_send,
    sum_recv,
    note_send,
    note_recv,
):
    inst, tp = lax.axis_index("inst"), lax.axis_index("tp")
    core = tp % 2
    other = flipped(tp, 1)
    partner = flipped(inst, mask)
    stay = query_stay.shape[0]
    page_count, _, page, _ = pool.shape
    half = out_pages.shape[0]

    part = page_count // PARTS
    loads = [
        pltpu.make_async_copy(
            kv_ref.at[pl.ds(c * part, part), 0], pool.at[pl.ds(c * part, part)], pool_sem.at[c]
        )
        for c in range(PARTS)
    ]
    for load in loads:
        load.start()

    barrier = pltpu.get_barrier_semaphore()
    pl.semaphore_signal(barrier, inc=1, device_id=(partner, tp), device_id_type=MESH)
    for b in range(tp_bits):
        pl.semaphore_signal(
            barrier, inc=1, device_id=(inst, flipped(tp, 1 << b)), device_id_type=MESH
        )

    queries[...] = jnp.zeros_like(queries)
    rows[...] = jnp.zeros_like(rows)
    stay_q, mig_q = query_stay[...].astype(jnp.float32), query_mig[...].astype(jnp.float32)
    for r in range(stay + 1):
        line = mig_q if r == stay else stay_q[r : r + 1]
        for h in range(GROUP):
            queries[r, h : h + 1, :] = line[:, h * LANES : (h + 1) * LANES]
    rows[0:stay, :] = hidden_stay[...].astype(jnp.float32)
    rows[stay : stay + 1, :] = hidden_mig[...].astype(jnp.float32)
    square = rows[...] * rows[...]
    width = square.shape[1]
    sums_out[0] = sum(square[:, c : c + LANES] for c in range(0, width, LANES))

    for load in loads:
        load.wait()
    pl.semaphore_wait(barrier, tp_bits + 1)

    length = len_mig[0]
    new_line = new_mig[0, 0]
    position = lax.broadcasted_iota(jnp.int32, (page, LANES), 0)
    sends = []
    for j in range(half):
        at = mig_table[0, core * half + j]
        here = position == length - 1 - (core * half + j) * page
        for k in range(2):
            out_pages[j, k] = jnp.where(here, new_line[k : k + 1], pool[at, k])
        send = pltpu.make_async_remote_copy(
            src_ref=out_pages.at[j],
            dst_ref=arrived.at[0, core * half + j, 0],
            send_sem=page_send.at[j],
            recv_sem=page_recv.at[j],
            device_id=(partner, tp),
            device_id_type=MESH,
        )
        send.start()
        sends.append(send)

    def sum_step(b):
        bit = 1 << b
        return pltpu.make_async_remote_copy(
            src_ref=sums_out.at[b],
            dst_ref=sums_in.at[b],
            send_sem=sum_send.at[b],
            recv_sem=sum_recv.at[b],
            device_id=(inst, flipped(tp, bit)),
            device_id_type=MESH,
        )

    def attend_staying(r, _):
        mixed[r] = attend(
            pool, block_table, r, queries[r].astype(jnp.bfloat16), new_stay[r, 0], len_stay[r]
        )
        return 0

    step = sum_step(0)
    step.start()
    leaving = attend(
        pool, mig_table, 0, queries[stay].astype(jnp.bfloat16), new_line, length
    )
    step.wait()
    done = 0
    for b in range(1, tp_bits):
        sums_out[b] = sums_out[b - 1] + sums_in[b - 1]
        step = sum_step(b)
        step.start()
        upto = stay * b // (tp_bits - 1)
        lax.fori_loop(done, upto, attend_staying, 0)
        done = upto
        step.wait()
    sums = sums_out[tp_bits - 1] + sums_in[tp_bits - 1]
    mean_square = jnp.sum(sums, axis=1, keepdims=True) / D
    rows[...] = rows[...] * lax.rsqrt(mean_square + 1e-05) * gain[...].astype(jnp.float32)

    note_out[0:8, :] = leaving.astype(jnp.bfloat16)
    own = rows[stay : stay + 1, :]
    lines = [own[:, h * LANES : (h + 1) * LANES] for h in range(GROUP)]
    note_out[8:16, :] = jnp.concatenate(lines + lines, axis=0).astype(jnp.bfloat16)
    note = pltpu.make_async_remote_copy(
        src_ref=note_out,
        dst_ref=note_in,
        send_sem=note_send,
        recv_sem=note_recv,
        device_id=(partner, tp),
        device_id_type=MESH,
    )
    note.start()

    passes = []
    for j in range(half):
        sends[j].wait_recv()
        onward = pltpu.make_async_remote_copy(
            src_ref=arrived.at[0, core * half + j, 0],
            dst_ref=arrived.at[0, core * half + j, 0],
            send_sem=pass_send.at[j],
            recv_sem=pass_recv.at[j],
            device_id=(inst, other),
            device_id_type=MESH,
        )
        onward.start()
        passes.append(onward)

    note.wait()
    got = note_in[...].astype(jnp.float32)
    mixed[stay] = got[0:8]
    for h in range(GROUP):
        attended[:, h * LANES : (h + 1) * LANES] = mixed[:, h, :].astype(jnp.bfloat16)
        rows[stay : stay + 1, h * LANES : (h + 1) * LANES] = got[8 + h : 9 + h]
    normed[...] = rows[0 : stay + 1, :].astype(jnp.bfloat16)
    for send in sends:
        send.wait_send()
    for onward in passes:
        onward.wait()


def local(
    kv_pool,
    block_table,
    mig_table,
    query_stay,
    query_mig,
    new_stay,
    new_mig,
    len_stay,
    len_mig,
    hidden_stay,
    hidden_mig,
    norm_gain,
    partner_mask,
):
    page_count, _, _, page, head = kv_pool.shape
    stay, width = query_stay.shape
    slots = mig_table.shape[1]
    half = slots // 2
    tp_bits = lax.axis_size("tp").bit_length() - 1
    bf16, f32 = jnp.bfloat16, jnp.float32
    vmem = pl.BlockSpec(memory_space=pltpu.VMEM)
    smem = pl.BlockSpec(memory_space=pltpu.SMEM)
    dma = pltpu.SemaphoreType.DMA

    def matched(mask):
        return pl.pallas_call(
            functools.partial(kernel, mask, tp_bits),
            out_shape=(
                jax.ShapeDtypeStruct((stay + 1, width), bf16),
                jax.ShapeDtypeStruct((1, slots, 1, 2, page, head), bf16),
                jax.ShapeDtypeStruct((stay + 1, width), bf16),
            ),
            in_specs=[pl.BlockSpec(memory_space=pl.ANY)] + [smem] * 4 + [vmem] * 7,
            out_specs=(vmem, vmem, vmem),
            scratch_shapes=[
                pltpu.VMEM((page_count, 2, page, head), bf16),
                pltpu.VMEM((half, 2, page, head), bf16),
                pltpu.VMEM((stay + 1, 8, head), f32),
                pltpu.VMEM((stay + 1, 8, head), f32),
                pltpu.VMEM((8, width), f32),
                pltpu.VMEM((tp_bits, 8, LANES), f32),
                pltpu.VMEM((tp_bits, 8, LANES), f32),
                pltpu.VMEM((16, LANES), bf16),
                pltpu.VMEM((16, LANES), bf16),
                dma((PARTS,)),
                dma((half,)),
                dma((half,)),
                dma((half,)),
                dma((half,)),
                dma((tp_bits,)),
                dma((tp_bits,)),
                dma,
                dma,
            ],
            compiler_params=pltpu.CompilerParams(
                collective_id=mask - 1, has_side_effects=True, vmem_limit_bytes=32 * 1024 * 1024
            ),
            name="matched",
        )

    operands = (
        kv_pool,
        block_table,
        mig_table,
        len_stay,
        len_mig,
        query_stay,
        query_mig,
        new_stay,
        new_mig,
        hidden_stay,
        hidden_mig,
        norm_gain.reshape(1, -1),
    )
    branches = [
        lambda *args, mask=mask: tuple(matched(mask)(*args))
        for mask in range(1, lax.axis_size("inst"))
    ]
    return lax.switch(partner_mask[0] - 1, branches, *operands)


def solution(mesh):
    return jax.shard_map(
        local,
        mesh=mesh,
        in_specs=(
            P("inst", "tp", None, None, None),
            P("inst", None),
            P("inst", None),
            P("inst", "tp"),
            P("inst", "tp"),
            P("inst", "tp", None, None),
            P("inst", "tp", None, None),
            P("inst"),
            P("inst"),
            P("inst", "tp"),
            P("inst", "tp"),
            P("tp"),
            P(),
        ),
        out_specs=(P("inst", "tp"), P("inst", None, "tp", None, None, None), P("inst", "tp")),
        check_vma=False,
    )
```

```python
import functools

import jax
import jax.numpy as jnp
from jax import lax
from jax.experimental import pallas as pl
from jax.experimental.pallas import tpu as pltpu
from jax.sharding import PartitionSpec as P

MESH = pl.DeviceIdType.MESH
D = 8192
LANES = 128
GROUP = 4
PAGES = 8
FIRST, SECOND = 1, 4
PARTS = 1
STEPS = ((1, 8, 9), (2, 4, 6))


def flipped(index, mask):
    bit = 1
    total = index
    while bit <= mask:
        if mask & bit:
            total = total + bit - 2 * bit * ((index // bit) % 2)
        bit *= 2
    return total


def attend(pool, page_of, query, new_kv, length):
    page = pool.shape[2]
    places = [page_of(j) for j in range(PAGES)]
    new_key = new_kv[0:1].astype(jnp.float32)
    new_value = new_kv[1:2].astype(jnp.float32)
    scale = LANES ** (-0.5)
    new_score = jnp.sum(query.astype(jnp.float32) * new_key, axis=1, keepdims=True) * scale
    column = lax.broadcasted_iota(jnp.int32, (query.shape[0], page), 1)
    scores = []
    for j, place in enumerate(places):
        score = lax.dot_general(
            query, pool[place, 0], (((1,), (1,)), ((), ())), preferred_element_type=jnp.float32
        )
        score = score * scale
        position = column + j * page
        score = jnp.where(position == length - 1, new_score, score)
        scores.append(jnp.where(position < length, score, -1e30))
    highest = functools.reduce(jnp.maximum, scores)
    highest = jnp.max(highest, axis=1, keepdims=True)
    weights = [
        jnp.where(column + j * page < length, jnp.exp(s - highest), 0.0)
        for j, s in enumerate(scores)
    ]
    total = jnp.sum(functools.reduce(jnp.add, weights), axis=1, keepdims=True)
    mixed = jnp.zeros((query.shape[0], LANES), jnp.float32)
    last = jnp.zeros((query.shape[0], page), jnp.float32)
    for j, (w, place) in enumerate(zip(weights, places)):
        w = (w / total).astype(jnp.bfloat16).astype(jnp.float32)
        is_last = column + j * page == length - 1
        last = last + jnp.where(is_last, w, 0.0)
        w = jnp.where(is_last, 0.0, w).astype(jnp.bfloat16)
        mixed = mixed + jnp.dot(w, pool[place, 1], preferred_element_type=jnp.float32)
    return mixed + jnp.sum(last, axis=1, keepdims=True) * new_value


def kernel(
    mask,
    kv_hbm,
    block_table_hbm,
    mig_table_hbm,
    len_stay_hbm,
    len_mig_hbm,
    query_stay_hbm,
    query_mig_hbm,
    new_stay_hbm,
    new_mig_hbm,
    hidden_stay_hbm,
    hidden_mig_hbm,
    gain_hbm,
    attended,
    arrived,
    normed,
    pool,
    block_table,
    mig_table,
    len_stay,
    len_mig,
    query_stay,
    query_mig,
    new_lines,
    hidden_stay,
    hidden_mig,
    gain,
    out_pages,
    queries,
    mixed,
    rows,
    sums_out,
    sums_in,
    note_out,
    note_in,
    pool_sem,
    load_sem,
    page_send,
    page_recv,
    pass_send,
    pass_recv,
    sum_send,
    sum_recv,
    note_send,
    note_recv,
):
    inst, tp = lax.axis_index("inst"), lax.axis_index("tp")
    core = tp % 2
    other = flipped(tp, 1)
    partner = flipped(inst, mask)
    stay = query_stay.shape[0]
    page_count, _, page, _ = pool.shape
    half = out_pages.shape[0]

    barrier = pltpu.get_barrier_semaphore()
    pl.semaphore_signal(barrier, inc=1, device_id=(partner, tp), device_id_type=MESH)
    for bits in STEPS[0] + STEPS[1]:
        pl.semaphore_signal(
            barrier, inc=1, device_id=(inst, flipped(tp, bits)), device_id_type=MESH
        )

    part = page_count // PARTS
    pool_loads = [
        pltpu.make_async_copy(
            kv_hbm.at[pl.ds(c * part, part), 0], pool.at[pl.ds(c * part, part)], pool_sem.at[c]
        )
        for c in range(PARTS)
    ]
    pairs = [
        (hidden_stay_hbm, hidden_stay),
        (hidden_mig_hbm, hidden_mig),
        (mig_table_hbm, mig_table),
        (len_mig_hbm, len_mig),
        (new_mig_hbm.at[:, 0], new_lines.at[pl.ds(stay, 1)]),
        (query_stay_hbm, query_stay),
        (query_mig_hbm, query_mig),
        (block_table_hbm, block_table),
        (len_stay_hbm, len_stay),
        (new_stay_hbm.at[:, 0], new_lines.at[pl.ds(0, stay)]),
        (gain_hbm, gain),
    ]
    small_loads = [
        pltpu.make_async_copy(src, dst, load_sem.at[c]) for c, (src, dst) in enumerate(pairs)
    ]
    for load in small_loads[:5]:
        load.start()
    for load in pool_loads:
        load.start()
    for load in small_loads[5:]:
        load.start()

    rows[...] = jnp.zeros_like(rows)
    for load in small_loads[:2]:
        load.wait()
    rows[0:stay, :] = hidden_stay[...].astype(jnp.float32)
    rows[stay : stay + 1, :] = hidden_mig[...].astype(jnp.float32)
    square = rows[...] * rows[...]
    width = square.shape[1]
    sums_out[0] = sum(square[:, c : c + LANES] for c in range(0, width, LANES))

    def sum_copies(step):
        return [
            pltpu.make_async_remote_copy(
                src_ref=sums_out.at[step],
                dst_ref=sums_in.at[step, c],
                send_sem=sum_send.at[step, c],
                recv_sem=sum_recv.at[step, c],
                device_id=(inst, flipped(tp, bits)),
                device_id_type=MESH,
            )
            for c, bits in enumerate(STEPS[step])
        ]

    def summed(step):
        copies = sum_copies(step)
        for copy in copies:
            copy.wait()
        return sums_out[step] + sum(sums_in[step, c] for c in range(len(copies)))

    def page_copy(j):
        return pltpu.make_async_remote_copy(
            src_ref=out_pages.at[j],
            dst_ref=arrived.at[0, core * half + j, 0],
            send_sem=page_send.at[j],
            recv_sem=page_recv.at[j],
            device_id=(partner, tp),
            device_id_type=MESH,
        )

    pl.semaphore_wait(barrier, 1 + len(STEPS[0] + STEPS[1]))
    for copy in sum_copies(0):
        copy.start()

    for load in small_loads[2:5] + pool_loads:
        load.wait()
    length = len_mig[0]
    new_line = new_lines[stay]
    position = lax.broadcasted_iota(jnp.int32, (page, LANES), 0)

    def send_page(j, _):
        at = mig_table[0, core * half + j]
        here = position == length - 1 - (core * half + j) * page
        for k in range(2):
            out_pages[j, k] = jnp.where(here, new_line[k : k + 1], pool[at, k])
        page_copy(j).start()
        return 0

    lax.fori_loop(0, half, send_page, 0)

    for load in small_loads[5:]:
        load.wait()
    queries[...] = jnp.zeros_like(queries)
    stay_q, mig_q = query_stay[...].astype(jnp.float32), query_mig[...].astype(jnp.float32)
    for h in range(GROUP):
        queries[0:stay, h, :] = stay_q[:, h * LANES : (h + 1) * LANES]
        queries[stay, h : h + 1, :] = mig_q[:, h * LANES : (h + 1) * LANES]

    own = stay
    note = pltpu.make_async_remote_copy(
        src_ref=note_out,
        dst_ref=note_in,
        send_sem=note_send,
        recv_sem=note_recv,
        device_id=(partner, tp),
        device_id_type=MESH,
    )

    def attend_next(i, _):
        r = own - i
        staying = jnp.minimum(r, stay - 1)

        def page_of(j):
            return jnp.where(r == own, mig_table[0, j], block_table[staying, j])

        mixed[r] = attend(
            pool,
            page_of,
            queries[r].astype(jnp.bfloat16),
            new_lines[r],
            jnp.where(r == own, length, len_stay[staying]),
        )

        @pl.when(i == FIRST)
        def _():
            sums_out[1] = summed(0)
            for copy in sum_copies(1):
                copy.start()

        @pl.when(i == SECOND)
        def _():
            sums = summed(1)
            mean_square = jnp.sum(sums, axis=1, keepdims=True) / D
            scaled = rows[...] * lax.rsqrt(mean_square + 1e-05)
            rows[...] = scaled * gain[...].astype(jnp.float32)[None, :]
            line = rows[own : own + 1, :]
            lines = [line[:, h * LANES : (h + 1) * LANES] for h in range(GROUP)]
            note_out[0:8, :] = mixed[own].astype(jnp.bfloat16)
            note_out[8:16, :] = jnp.concatenate(lines + lines, axis=0).astype(jnp.bfloat16)
            note.start()

        return 0

    lax.fori_loop(0, stay + 1, attend_next, 0)

    def pass_copy(j):
        return pltpu.make_async_remote_copy(
            src_ref=arrived.at[0, core * half + j, 0],
            dst_ref=arrived.at[0, core * half + j, 0],
            send_sem=pass_send.at[j],
            recv_sem=pass_recv.at[j],
            device_id=(inst, other),
            device_id_type=MESH,
        )

    def pass_on(j, _):
        page_copy(j).wait_recv()
        pass_copy(j).start()
        return 0

    lax.fori_loop(0, half, pass_on, 0)

    note.wait()
    got = note_in[...].astype(jnp.float32)
    mixed[stay] = got[0:8]
    for h in range(GROUP):
        attended[:, h * LANES : (h + 1) * LANES] = mixed[:, h, :].astype(jnp.bfloat16)
        rows[stay : stay + 1, h * LANES : (h + 1) * LANES] = got[8 + h : 9 + h]
    normed[...] = rows[0 : stay + 1, :].astype(jnp.bfloat16)

    def finish(j, _):
        page_copy(j).wait_send()
        pass_copy(j).wait()
        return 0

    lax.fori_loop(0, half, finish, 0)


def settle(*refs):
    count = (len(refs) - 1) // 2
    copies = [
        pltpu.make_async_copy(refs[c], refs[count + c], refs[-1].at[c]) for c in range(count)
    ]
    for copy in copies:
        copy.start()
    for copy in copies:
        copy.wait()


def local(
    kv_pool,
    block_table,
    mig_table,
    query_stay,
    query_mig,
    new_stay,
    new_mig,
    len_stay,
    len_mig,
    hidden_stay,
    hidden_mig,
    norm_gain,
    partner_mask,
):
    page_count, _, _, page, head = kv_pool.shape
    stay, width = query_stay.shape
    slots = mig_table.shape[1]
    half = slots // 2
    bf16, f32 = jnp.bfloat16, jnp.float32
    vmem = pl.BlockSpec(memory_space=pltpu.VMEM)
    anywhere = pl.BlockSpec(memory_space=pl.ANY)
    dma = pltpu.SemaphoreType.DMA

    operands = (
        kv_pool,
        block_table,
        mig_table,
        len_stay,
        len_mig,
        query_stay,
        query_mig,
        new_stay,
        new_mig,
        hidden_stay,
        hidden_mig,
        norm_gain,
    )
    results = (
        jax.ShapeDtypeStruct((stay + 1, width), bf16),
        jax.ShapeDtypeStruct((1, slots, 1, 2, page, head), bf16),
        jax.ShapeDtypeStruct((stay + 1, width), bf16),
    )

    def matched(mask):
        return pl.pallas_call(
            functools.partial(kernel, mask),
            out_shape=results,
            in_specs=[anywhere] * len(operands),
            out_specs=(vmem, vmem, vmem),
            scratch_shapes=[
                pltpu.VMEM((page_count, 2, page, head), bf16),
                *(pltpu.SMEM(a.shape, a.dtype) for a in operands[1:5]),
                *(pltpu.VMEM(a.shape, a.dtype) for a in operands[5:7]),
                pltpu.VMEM((stay + 1, 2, head), bf16),
                *(pltpu.VMEM(a.shape, a.dtype) for a in operands[9:]),
                pltpu.VMEM((half, 2, page, head), bf16),
                pltpu.VMEM((stay + 1, 8, head), f32),
                pltpu.VMEM((stay + 1, 8, head), f32),
                pltpu.VMEM((8, width), f32),
                pltpu.VMEM((2, 8, LANES), f32),
                pltpu.VMEM((2, 3, 8, LANES), f32),
                pltpu.VMEM((16, LANES), bf16),
                pltpu.VMEM((16, LANES), bf16),
                dma((PARTS,)),
                dma((len(operands) - 1,)),
                dma((half,)),
                dma((half,)),
                dma((half,)),
                dma((half,)),
                dma((2, 3)),
                dma((2, 3)),
                dma,
                dma,
            ],
            compiler_params=pltpu.CompilerParams(
                collective_id=mask - 1, has_side_effects=True, vmem_limit_bytes=32 * 1024 * 1024
            ),
            name="matched",
        )

    branches = [
        lambda *args, mask=mask: tuple(matched(mask)(*args))
        for mask in range(1, lax.axis_size("inst"))
    ]
    found = lax.switch(partner_mask[0] - 1, branches, *operands)
    return pl.pallas_call(
        settle,
        out_shape=results,
        in_specs=[vmem] * 3,
        out_specs=(anywhere,) * 3,
        scratch_shapes=[dma((3,))],
        compiler_params=pltpu.CompilerParams(vmem_limit_bytes=4 * 1024 * 1024),
        name="settle",
    )(*found)


def solution(mesh):
    return jax.shard_map(
        local,
        mesh=mesh,
        in_specs=(
            P("inst", "tp", None, None, None),
            P("inst", None),
            P("inst", None),
            P("inst", "tp"),
            P("inst", "tp"),
            P("inst", "tp", None, None),
            P("inst", "tp", None, None),
            P("inst"),
            P("inst"),
            P("inst", "tp"),
            P("inst", "tp"),
            P("tp"),
            P(),
        ),
        out_specs=(P("inst", "tp"), P("inst", None, "tp", None, None, None), P("inst", "tp")),
        check_vma=False,
    )
```

```python
import functools

import jax
import jax.numpy as jnp
from jax import lax
from jax.experimental import pallas as pl
from jax.experimental.pallas import tpu as pltpu
from jax.sharding import PartitionSpec as P

MESH = pl.DeviceIdType.MESH
D = 8192
LANES = 128
GROUP = 4
PAGES = 8
FIRST, SECOND = 1, 4
PARTS = 1
STEPS = ((1, 8, 9), (2, 4, 6))


def flipped(index, mask):
    bit = 1
    total = index
    while bit <= mask:
        if mask & bit:
            total = total + bit - 2 * bit * ((index // bit) % 2)
        bit *= 2
    return total


def greets_first(tp, bits):
    top = 1 << (bits.bit_length() - 1)
    side = tp // top % 2
    return side if bits == 1 else 1 - side


def attend(pool, page_of, query, new_kv, length):
    page = pool.shape[2]
    places = [page_of(j) for j in range(PAGES)]
    new_key = new_kv[0:1].astype(jnp.float32)
    new_value = new_kv[1:2].astype(jnp.float32)
    scale = LANES ** (-0.5)
    new_score = jnp.sum(query.astype(jnp.float32) * new_key, axis=1, keepdims=True) * scale
    column = lax.broadcasted_iota(jnp.int32, (query.shape[0], page), 1)
    scores = []
    for j, place in enumerate(places):
        score = lax.dot_general(
            query, pool[place, 0], (((1,), (1,)), ((), ())), preferred_element_type=jnp.float32
        )
        score = score * scale
        position = column + j * page
        score = jnp.where(position == length - 1, new_score, score)
        scores.append(jnp.where(position < length, score, -1e30))
    highest = functools.reduce(jnp.maximum, scores)
    highest = jnp.max(highest, axis=1, keepdims=True)
    weights = [
        jnp.where(column + j * page < length, jnp.exp(s - highest), 0.0)
        for j, s in enumerate(scores)
    ]
    total = jnp.sum(functools.reduce(jnp.add, weights), axis=1, keepdims=True)
    mixed = jnp.zeros((query.shape[0], LANES), jnp.float32)
    last = jnp.zeros((query.shape[0], page), jnp.float32)
    for j, (w, place) in enumerate(zip(weights, places)):
        w = (w / total).astype(jnp.bfloat16).astype(jnp.float32)
        is_last = column + j * page == length - 1
        last = last + jnp.where(is_last, w, 0.0)
        w = jnp.where(is_last, 0.0, w).astype(jnp.bfloat16)
        mixed = mixed + jnp.dot(w, pool[place, 1], preferred_element_type=jnp.float32)
    return mixed + jnp.sum(last, axis=1, keepdims=True) * new_value


def kernel(
    mask,
    kv_hbm,
    block_table_hbm,
    mig_table_hbm,
    len_stay_hbm,
    len_mig_hbm,
    query_stay_hbm,
    query_mig_hbm,
    new_stay_hbm,
    new_mig_hbm,
    hidden_stay_hbm,
    hidden_mig_hbm,
    gain_hbm,
    attended,
    arrived,
    normed,
    pool,
    block_table,
    mig_table,
    len_stay,
    len_mig,
    query_stay,
    query_mig,
    new_lines,
    hidden_stay,
    hidden_mig,
    gain,
    out_pages,
    queries,
    mixed,
    rows,
    sums_out,
    sums_in,
    note_out,
    note_in,
    pool_sem,
    load_sem,
    page_send,
    page_recv,
    pass_send,
    pass_recv,
    sum_send,
    sum_recv,
    note_send,
    note_recv,
    answer_sem,
):
    inst, tp = lax.axis_index("inst"), lax.axis_index("tp")
    core = tp % 2
    other = flipped(tp, 1)
    partner = flipped(inst, mask)
    stay = query_stay.shape[0]
    page_count, _, page, _ = pool.shape
    half = out_pages.shape[0]

    barrier = pltpu.get_barrier_semaphore()
    pl.semaphore_signal(barrier, inc=1, device_id=(partner, tp), device_id_type=MESH)
    others = STEPS[0] + STEPS[1]
    far = mask % 16 >= 4
    answers = 0
    for bits in others:
        first = greets_first(tp, bits) if far else 1
        answers = answers + first

        @pl.when(first == 1)
        def _(bits=bits):
            pl.semaphore_signal(
                barrier, inc=1, device_id=(inst, flipped(tp, bits)), device_id_type=MESH
            )

    part = page_count // PARTS
    pool_loads = [
        pltpu.make_async_copy(
            kv_hbm.at[pl.ds(c * part, part), 0], pool.at[pl.ds(c * part, part)], pool_sem.at[c]
        )
        for c in range(PARTS)
    ]
    pairs = [
        (hidden_stay_hbm, hidden_stay),
        (hidden_mig_hbm, hidden_mig),
        (mig_table_hbm, mig_table),
        (len_mig_hbm, len_mig),
        (new_mig_hbm.at[:, 0], new_lines.at[pl.ds(stay, 1)]),
        (query_stay_hbm, query_stay),
        (query_mig_hbm, query_mig),
        (block_table_hbm, block_table),
        (len_stay_hbm, len_stay),
        (new_stay_hbm.at[:, 0], new_lines.at[pl.ds(0, stay)]),
        (gain_hbm, gain),
    ]
    small_loads = [
        pltpu.make_async_copy(src, dst, load_sem.at[c]) for c, (src, dst) in enumerate(pairs)
    ]
    for load in small_loads[:5]:
        load.start()
    for load in pool_loads:
        load.start()
    for load in small_loads[5:]:
        load.start()

    rows[...] = jnp.zeros_like(rows)
    for load in small_loads[:2]:
        load.wait()
    rows[0:stay, :] = hidden_stay[...].astype(jnp.float32)
    rows[stay : stay + 1, :] = hidden_mig[...].astype(jnp.float32)
    square = rows[...] * rows[...]
    width = square.shape[1]
    sums_out[0] = sum(square[:, c : c + LANES] for c in range(0, width, LANES))

    def sum_copies(step):
        return [
            pltpu.make_async_remote_copy(
                src_ref=sums_out.at[step],
                dst_ref=sums_in.at[step, c],
                send_sem=sum_send.at[step, c],
                recv_sem=sum_recv.at[step, c],
                device_id=(inst, flipped(tp, bits)),
                device_id_type=MESH,
            )
            for c, bits in enumerate(STEPS[step])
        ]

    def summed(step):
        copies = sum_copies(step)
        for copy in copies:
            copy.wait()
        return sums_out[step] + sum(sums_in[step, c] for c in range(len(copies)))

    def page_copy(j):
        return pltpu.make_async_remote_copy(
            src_ref=out_pages.at[j],
            dst_ref=arrived.at[0, core * half + j, 0],
            send_sem=page_send.at[j],
            recv_sem=page_recv.at[j],
            device_id=(partner, tp),
            device_id_type=MESH,
        )

    def start_sums(step):
        for copy in sum_copies(step):
            copy.start()

    if far:
        pl.semaphore_wait(barrier, 1 + len(others) - answers)
        for bits in others:

            @pl.when(greets_first(tp, bits) == 0)
            def _(bits=bits):
                pl.semaphore_signal(
                    answer_sem, inc=1, device_id=(inst, flipped(tp, bits)), device_id_type=MESH
                )

    else:
        pl.semaphore_wait(barrier, 1 + len(others))
        start_sums(0)

    for load in small_loads[2:5] + pool_loads:
        load.wait()
    length = len_mig[0]
    new_line = new_lines[stay]
    position = lax.broadcasted_iota(jnp.int32, (page, LANES), 0)

    def send_page(j, _):
        at = mig_table[0, core * half + j]
        here = position == length - 1 - (core * half + j) * page
        for k in range(2):
            out_pages[j, k] = jnp.where(here, new_line[k : k + 1], pool[at, k])
        page_copy(j).start()
        return 0

    held = half * (inst // 4 % 2) if mask // 4 % 4 == 2 else 0
    lax.fori_loop(0, half - held, send_page, 0)
    if far:

        @pl.when(answers > 0)
        def _():
            pl.semaphore_wait(answer_sem, answers)

        start_sums(0)

    for load in small_loads[5:]:
        load.wait()
    queries[...] = jnp.zeros_like(queries)
    stay_q, mig_q = query_stay[...].astype(jnp.float32), query_mig[...].astype(jnp.float32)
    for h in range(GROUP):
        queries[0:stay, h, :] = stay_q[:, h * LANES : (h + 1) * LANES]
        queries[stay, h : h + 1, :] = mig_q[:, h * LANES : (h + 1) * LANES]

    own = stay
    note = pltpu.make_async_remote_copy(
        src_ref=note_out,
        dst_ref=note_in,
        send_sem=note_send,
        recv_sem=note_recv,
        device_id=(partner, tp),
        device_id_type=MESH,
    )

    def attend_next(i, _):
        r = own - i
        staying = jnp.minimum(r, stay - 1)

        def page_of(j):
            return jnp.where(r == own, mig_table[0, j], block_table[staying, j])

        mixed[r] = attend(
            pool,
            page_of,
            queries[r].astype(jnp.bfloat16),
            new_lines[r],
            jnp.where(r == own, length, len_stay[staying]),
        )

        @pl.when(i == 0)
        def _():
            if mask // 4 % 4 == 2:
                lax.fori_loop(half - held, half, send_page, 0)

        @pl.when(i == FIRST)
        def _():
            sums_out[1] = summed(0)
            start_sums(1)

        @pl.when(i == SECOND)
        def _():
            sums = summed(1)
            mean_square = jnp.sum(sums, axis=1, keepdims=True) / D
            scaled = rows[...] * lax.rsqrt(mean_square + 1e-05)
            rows[...] = scaled * gain[...].astype(jnp.float32)[None, :]
            line = rows[own : own + 1, :]
            lines = [line[:, h * LANES : (h + 1) * LANES] for h in range(GROUP)]
            note_out[0:8, :] = mixed[own].astype(jnp.bfloat16)
            note_out[8:16, :] = jnp.concatenate(lines + lines, axis=0).astype(jnp.bfloat16)
            note.start()

        return 0

    lax.fori_loop(0, stay + 1, attend_next, 0)

    def pass_copy(j):
        return pltpu.make_async_remote_copy(
            src_ref=arrived.at[0, core * half + j, 0],
            dst_ref=arrived.at[0, core * half + j, 0],
            send_sem=pass_send.at[j],
            recv_sem=pass_recv.at[j],
            device_id=(inst, other),
            device_id_type=MESH,
        )

    def pass_on(j, _):
        page_copy(j).wait_recv()
        pass_copy(j).start()
        return 0

    lax.fori_loop(0, half, pass_on, 0)

    note.wait()
    got = note_in[...].astype(jnp.float32)
    mixed[stay] = got[0:8]
    for h in range(GROUP):
        attended[:, h * LANES : (h + 1) * LANES] = mixed[:, h, :].astype(jnp.bfloat16)
        rows[stay : stay + 1, h * LANES : (h + 1) * LANES] = got[8 + h : 9 + h]
    normed[...] = rows[0 : stay + 1, :].astype(jnp.bfloat16)

    def finish(j, _):
        page_copy(j).wait_send()
        pass_copy(j).wait()
        return 0

    lax.fori_loop(0, half, finish, 0)


def settle(*refs):
    count = (len(refs) - 1) // 2
    copies = [
        pltpu.make_async_copy(refs[c], refs[count + c], refs[-1].at[c]) for c in range(count)
    ]
    for copy in copies:
        copy.start()
    for copy in copies:
        copy.wait()


def local(
    kv_pool,
    block_table,
    mig_table,
    query_stay,
    query_mig,
    new_stay,
    new_mig,
    len_stay,
    len_mig,
    hidden_stay,
    hidden_mig,
    norm_gain,
    partner_mask,
):
    page_count, _, _, page, head = kv_pool.shape
    stay, width = query_stay.shape
    slots = mig_table.shape[1]
    half = slots // 2
    bf16, f32 = jnp.bfloat16, jnp.float32
    vmem = pl.BlockSpec(memory_space=pltpu.VMEM)
    anywhere = pl.BlockSpec(memory_space=pl.ANY)
    dma = pltpu.SemaphoreType.DMA

    operands = (
        kv_pool,
        block_table,
        mig_table,
        len_stay,
        len_mig,
        query_stay,
        query_mig,
        new_stay,
        new_mig,
        hidden_stay,
        hidden_mig,
        norm_gain,
    )
    results = (
        jax.ShapeDtypeStruct((stay + 1, width), bf16),
        jax.ShapeDtypeStruct((1, slots, 1, 2, page, head), bf16),
        jax.ShapeDtypeStruct((stay + 1, width), bf16),
    )

    def matched(mask):
        return pl.pallas_call(
            functools.partial(kernel, mask),
            out_shape=results,
            in_specs=[anywhere] * len(operands),
            out_specs=(vmem, vmem, vmem),
            scratch_shapes=[
                pltpu.VMEM((page_count, 2, page, head), bf16),
                *(pltpu.SMEM(a.shape, a.dtype) for a in operands[1:5]),
                *(pltpu.VMEM(a.shape, a.dtype) for a in operands[5:7]),
                pltpu.VMEM((stay + 1, 2, head), bf16),
                *(pltpu.VMEM(a.shape, a.dtype) for a in operands[9:]),
                pltpu.VMEM((half, 2, page, head), bf16),
                pltpu.VMEM((stay + 1, 8, head), f32),
                pltpu.VMEM((stay + 1, 8, head), f32),
                pltpu.VMEM((8, width), f32),
                pltpu.VMEM((2, 8, LANES), f32),
                pltpu.VMEM((2, 3, 8, LANES), f32),
                pltpu.VMEM((16, LANES), bf16),
                pltpu.VMEM((16, LANES), bf16),
                dma((PARTS,)),
                dma((len(operands) - 1,)),
                dma((half,)),
                dma((half,)),
                dma((half,)),
                dma((half,)),
                dma((2, 3)),
                dma((2, 3)),
                dma,
                dma,
                pltpu.SemaphoreType.REGULAR,
            ],
            compiler_params=pltpu.CompilerParams(
                collective_id=mask - 1, has_side_effects=True, vmem_limit_bytes=32 * 1024 * 1024
            ),
            name="matched",
        )

    branches = [
        lambda *args, mask=mask: tuple(matched(mask)(*args))
        for mask in range(1, lax.axis_size("inst"))
    ]
    found = lax.switch(partner_mask[0] - 1, branches, *operands)
    return pl.pallas_call(
        settle,
        out_shape=results,
        in_specs=[vmem] * 3,
        out_specs=(anywhere,) * 3,
        scratch_shapes=[dma((3,))],
        compiler_params=pltpu.CompilerParams(vmem_limit_bytes=4 * 1024 * 1024),
        name="settle",
    )(*found)


def solution(mesh):
    return jax.shard_map(
        local,
        mesh=mesh,
        in_specs=(
            P("inst", "tp", None, None, None),
            P("inst", None),
            P("inst", None),
            P("inst", "tp"),
            P("inst", "tp"),
            P("inst", "tp", None, None),
            P("inst", "tp", None, None),
            P("inst"),
            P("inst"),
            P("inst", "tp"),
            P("inst", "tp"),
            P("tp"),
            P(),
        ),
        out_specs=(P("inst", "tp"), P("inst", None, "tp", None, None, None), P("inst", "tp")),
        check_vma=False,
    )
```

```python
import functools

import jax
import jax.numpy as jnp
from jax import lax
from jax.experimental import pallas as pl
from jax.experimental.pallas import tpu as pltpu
from jax.sharding import PartitionSpec as P

MESH = pl.DeviceIdType.MESH
D = 8192
LANES = 128
GROUP = 4
PAGES = 8
FIRST, SECOND = 1, 4
PARTS = 1
STEPS = ((1, 8, 9), (2, 4, 6))


def flipped(index, mask):
    bit = 1
    total = index
    while bit <= mask:
        if mask & bit:
            total = total + bit - 2 * bit * ((index // bit) % 2)
        bit *= 2
    return total


def greets_first(tp, bits):
    top = 1 << (bits.bit_length() - 1)
    side = tp // top % 2
    return side if bits == 1 else 1 - side


def attend(pool, page_of, query, new_kv, length):
    page = pool.shape[2]
    places = [page_of(j) for j in range(PAGES)]
    new_key = new_kv[0:1].astype(jnp.float32)
    new_value = new_kv[1:2].astype(jnp.float32)
    scale = LANES ** (-0.5)
    new_score = jnp.sum(query.astype(jnp.float32) * new_key, axis=1, keepdims=True) * scale
    column = lax.broadcasted_iota(jnp.int32, (query.shape[0], page), 1)
    scores = []
    for j, place in enumerate(places):
        score = lax.dot_general(
            query, pool[place, 0], (((1,), (1,)), ((), ())), preferred_element_type=jnp.float32
        )
        score = score * scale
        position = column + j * page
        score = jnp.where(position == length - 1, new_score, score)
        scores.append(jnp.where(position < length, score, -1e30))
    highest = functools.reduce(jnp.maximum, scores)
    highest = jnp.max(highest, axis=1, keepdims=True)
    weights = [
        jnp.where(column + j * page < length, jnp.exp(s - highest), 0.0)
        for j, s in enumerate(scores)
    ]
    total = jnp.sum(functools.reduce(jnp.add, weights), axis=1, keepdims=True)
    mixed = jnp.zeros((query.shape[0], LANES), jnp.float32)
    last = jnp.zeros((query.shape[0], page), jnp.float32)
    for j, (w, place) in enumerate(zip(weights, places)):
        w = (w / total).astype(jnp.bfloat16).astype(jnp.float32)
        is_last = column + j * page == length - 1
        last = last + jnp.where(is_last, w, 0.0)
        w = jnp.where(is_last, 0.0, w).astype(jnp.bfloat16)
        mixed = mixed + jnp.dot(w, pool[place, 1], preferred_element_type=jnp.float32)
    return mixed + jnp.sum(last, axis=1, keepdims=True) * new_value


def kernel(
    mask,
    kv_hbm,
    block_table_hbm,
    mig_table_hbm,
    len_stay_hbm,
    len_mig_hbm,
    query_stay_hbm,
    query_mig_hbm,
    new_stay_hbm,
    new_mig_hbm,
    hidden_stay_hbm,
    hidden_mig_hbm,
    gain_hbm,
    attended,
    arrived,
    normed,
    pool,
    block_table,
    mig_table,
    len_stay,
    len_mig,
    query_stay,
    query_mig,
    new_lines,
    hidden_stay,
    hidden_mig,
    gain,
    out_pages,
    queries,
    mixed,
    rows,
    sums_out,
    sums_in,
    note_out,
    note_in,
    pool_sem,
    load_sem,
    page_send,
    page_recv,
    pass_send,
    pass_recv,
    sum_send,
    sum_recv,
    note_send,
    note_recv,
    answer_sem,
):
    inst, tp = lax.axis_index("inst"), lax.axis_index("tp")
    core = tp % 2
    other = flipped(tp, 1)
    partner = flipped(inst, mask)
    stay = query_stay.shape[0]
    page_count, _, page, _ = pool.shape
    half = out_pages.shape[0]

    part = page_count // PARTS
    pool_loads = [
        pltpu.make_async_copy(
            kv_hbm.at[pl.ds(c * part, part), 0], pool.at[pl.ds(c * part, part)], pool_sem.at[c]
        )
        for c in range(PARTS)
    ]
    pairs = [
        (hidden_stay_hbm, hidden_stay),
        (hidden_mig_hbm, hidden_mig),
        (mig_table_hbm, mig_table),
        (len_mig_hbm, len_mig),
        (new_mig_hbm.at[:, 0], new_lines.at[pl.ds(stay, 1)]),
        (query_stay_hbm, query_stay),
        (query_mig_hbm, query_mig),
        (block_table_hbm, block_table),
        (len_stay_hbm, len_stay),
        (new_stay_hbm.at[:, 0], new_lines.at[pl.ds(0, stay)]),
        (gain_hbm, gain),
    ]
    small_loads = [
        pltpu.make_async_copy(src, dst, load_sem.at[c]) for c, (src, dst) in enumerate(pairs)
    ]
    for load in pool_loads + small_loads[:5]:
        load.start()

    barrier = pltpu.get_barrier_semaphore()
    pl.semaphore_signal(barrier, inc=1, device_id=(partner, tp), device_id_type=MESH)
    steps = STEPS[::-1] if mask in (17, 19) else STEPS
    others = steps[0] + steps[1]
    far = mask % 16 >= 4 or mask in (2, 3)
    answers = 0
    for bits in others:
        first = greets_first(tp, bits) if far else 1
        answers = answers + first

        @pl.when(first == 1)
        def _(bits=bits):
            pl.semaphore_signal(
                barrier, inc=1, device_id=(inst, flipped(tp, bits)), device_id_type=MESH
            )

    for load in small_loads[5:]:
        load.start()

    rows[...] = jnp.zeros_like(rows)
    for load in small_loads[:2]:
        load.wait()
    rows[0:stay, :] = hidden_stay[...].astype(jnp.float32)
    rows[stay : stay + 1, :] = hidden_mig[...].astype(jnp.float32)
    square = rows[...] * rows[...]
    width = square.shape[1]
    sums_out[0] = sum(square[:, c : c + LANES] for c in range(0, width, LANES))

    def sum_copies(step):
        return [
            pltpu.make_async_remote_copy(
                src_ref=sums_out.at[step],
                dst_ref=sums_in.at[step, c],
                send_sem=sum_send.at[step, c],
                recv_sem=sum_recv.at[step, c],
                device_id=(inst, flipped(tp, bits)),
                device_id_type=MESH,
            )
            for c, bits in enumerate(steps[step])
        ]

    def summed(step):
        copies = sum_copies(step)
        for copy in copies:
            copy.wait()
        return sums_out[step] + sum(sums_in[step, c] for c in range(len(copies)))

    def page_copy(j):
        return pltpu.make_async_remote_copy(
            src_ref=out_pages.at[j],
            dst_ref=arrived.at[0, core * half + j, 0],
            send_sem=page_send.at[j],
            recv_sem=page_recv.at[j],
            device_id=(partner, tp),
            device_id_type=MESH,
        )

    def start_sums(step):
        for copy in sum_copies(step):
            copy.start()

    if far:
        pl.semaphore_wait(barrier, 1 + len(others) - answers)
        for bits in others:

            @pl.when(greets_first(tp, bits) == 0)
            def _(bits=bits):
                pl.semaphore_signal(
                    answer_sem, inc=1, device_id=(inst, flipped(tp, bits)), device_id_type=MESH
                )

    else:
        pl.semaphore_wait(barrier, 1 + len(others))
        start_sums(0)

    for load in small_loads[2:5] + pool_loads:
        load.wait()
    length = len_mig[0]
    new_line = new_lines[stay]
    position = lax.broadcasted_iota(jnp.int32, (page, LANES), 0)

    def send_page(j, _):
        at = mig_table[0, core * half + j]
        here = position == length - 1 - (core * half + j) * page
        for k in range(2):
            out_pages[j, k] = jnp.where(here, new_line[k : k + 1], pool[at, k])
        page_copy(j).start()
        return 0

    held = half * (inst // 4 % 2) if mask // 4 % 4 == 2 else 0
    lax.fori_loop(0, half - held, send_page, 0)
    if far:

        @pl.when(answers > 0)
        def _():
            pl.semaphore_wait(answer_sem, answers)

        start_sums(0)

    for load in small_loads[5:]:
        load.wait()
    queries[...] = jnp.zeros_like(queries)
    stay_q, mig_q = query_stay[...].astype(jnp.float32), query_mig[...].astype(jnp.float32)
    for h in range(GROUP):
        queries[0:stay, h, :] = stay_q[:, h * LANES : (h + 1) * LANES]
        queries[stay, h : h + 1, :] = mig_q[:, h * LANES : (h + 1) * LANES]

    own = stay
    note = pltpu.make_async_remote_copy(
        src_ref=note_out,
        dst_ref=note_in,
        send_sem=note_send,
        recv_sem=note_recv,
        device_id=(partner, tp),
        device_id_type=MESH,
    )

    def attend_next(i, _):
        r = own - i
        staying = jnp.minimum(r, stay - 1)

        def page_of(j):
            return jnp.where(r == own, mig_table[0, j], block_table[staying, j])

        mixed[r] = attend(
            pool,
            page_of,
            queries[r].astype(jnp.bfloat16),
            new_lines[r],
            jnp.where(r == own, length, len_stay[staying]),
        )

        @pl.when(i == 0)
        def _():
            if mask // 4 % 4 == 2:
                lax.fori_loop(half - held, half, send_page, 0)

        @pl.when(i == FIRST)
        def _():
            sums_out[1] = summed(0)
            start_sums(1)

        @pl.when(i == SECOND)
        def _():
            sums = summed(1)
            mean_square = jnp.sum(sums, axis=1, keepdims=True) / D
            scaled = rows[...] * lax.rsqrt(mean_square + 1e-05)
            rows[...] = scaled * gain[...].astype(jnp.float32)[None, :]
            line = rows[own : own + 1, :]
            lines = [line[:, h * LANES : (h + 1) * LANES] for h in range(GROUP)]
            note_out[0:8, :] = mixed[own].astype(jnp.bfloat16)
            note_out[8:16, :] = jnp.concatenate(lines + lines, axis=0).astype(jnp.bfloat16)
            note.start()

        return 0

    lax.fori_loop(0, stay + 1, attend_next, 0)

    def pass_copy(j):
        return pltpu.make_async_remote_copy(
            src_ref=arrived.at[0, core * half + j, 0],
            dst_ref=arrived.at[0, core * half + j, 0],
            send_sem=pass_send.at[j],
            recv_sem=pass_recv.at[j],
            device_id=(inst, other),
            device_id_type=MESH,
        )

    def pass_on(j, _):
        page_copy(j).wait_recv()
        pass_copy(j).start()
        return 0

    lax.fori_loop(0, half, pass_on, 0)

    note.wait()
    got = note_in[...].astype(jnp.float32)
    mixed[stay] = got[0:8]
    for h in range(GROUP):
        attended[:, h * LANES : (h + 1) * LANES] = mixed[:, h, :].astype(jnp.bfloat16)
        rows[stay : stay + 1, h * LANES : (h + 1) * LANES] = got[8 + h : 9 + h]
    normed[...] = rows[0 : stay + 1, :].astype(jnp.bfloat16)

    def finish(j, _):
        page_copy(j).wait_send()
        pass_copy(j).wait()
        return 0

    lax.fori_loop(0, half, finish, 0)


def settle(*refs):
    count = (len(refs) - 1) // 2
    copies = [
        pltpu.make_async_copy(refs[c], refs[count + c], refs[-1].at[c]) for c in range(count)
    ]
    for copy in copies:
        copy.start()
    for copy in copies:
        copy.wait()


def local(
    kv_pool,
    block_table,
    mig_table,
    query_stay,
    query_mig,
    new_stay,
    new_mig,
    len_stay,
    len_mig,
    hidden_stay,
    hidden_mig,
    norm_gain,
    partner_mask,
):
    page_count, _, _, page, head = kv_pool.shape
    stay, width = query_stay.shape
    slots = mig_table.shape[1]
    half = slots // 2
    bf16, f32 = jnp.bfloat16, jnp.float32
    vmem = pl.BlockSpec(memory_space=pltpu.VMEM)
    anywhere = pl.BlockSpec(memory_space=pl.ANY)
    dma = pltpu.SemaphoreType.DMA

    operands = (
        kv_pool,
        block_table,
        mig_table,
        len_stay,
        len_mig,
        query_stay,
        query_mig,
        new_stay,
        new_mig,
        hidden_stay,
        hidden_mig,
        norm_gain,
    )
    results = (
        jax.ShapeDtypeStruct((stay + 1, width), bf16),
        jax.ShapeDtypeStruct((1, slots, 1, 2, page, head), bf16),
        jax.ShapeDtypeStruct((stay + 1, width), bf16),
    )

    def matched(mask):
        return pl.pallas_call(
            functools.partial(kernel, mask),
            out_shape=results,
            in_specs=[anywhere] * len(operands),
            out_specs=(vmem, vmem, vmem),
            scratch_shapes=[
                pltpu.VMEM((page_count, 2, page, head), bf16),
                *(pltpu.SMEM(a.shape, a.dtype) for a in operands[1:5]),
                *(pltpu.VMEM(a.shape, a.dtype) for a in operands[5:7]),
                pltpu.VMEM((stay + 1, 2, head), bf16),
                *(pltpu.VMEM(a.shape, a.dtype) for a in operands[9:]),
                pltpu.VMEM((half, 2, page, head), bf16),
                pltpu.VMEM((stay + 1, 8, head), f32),
                pltpu.VMEM((stay + 1, 8, head), f32),
                pltpu.VMEM((8, width), f32),
                pltpu.VMEM((2, 8, LANES), f32),
                pltpu.VMEM((2, 3, 8, LANES), f32),
                pltpu.VMEM((16, LANES), bf16),
                pltpu.VMEM((16, LANES), bf16),
                dma((PARTS,)),
                dma((len(operands) - 1,)),
                dma((half,)),
                dma((half,)),
                dma((half,)),
                dma((half,)),
                dma((2, 3)),
                dma((2, 3)),
                dma,
                dma,
                pltpu.SemaphoreType.REGULAR,
            ],
            compiler_params=pltpu.CompilerParams(
                collective_id=mask - 1, has_side_effects=True, vmem_limit_bytes=32 * 1024 * 1024
            ),
            name="matched",
        )

    branches = [
        lambda *args, mask=mask: tuple(matched(mask)(*args))
        for mask in range(1, lax.axis_size("inst"))
    ]
    found = lax.switch(partner_mask[0] - 1, branches, *operands)
    return pl.pallas_call(
        settle,
        out_shape=results,
        in_specs=[vmem] * 3,
        out_specs=(anywhere,) * 3,
        scratch_shapes=[dma((3,))],
        compiler_params=pltpu.CompilerParams(vmem_limit_bytes=4 * 1024 * 1024),
        name="settle",
    )(*found)


def solution(mesh):
    return jax.shard_map(
        local,
        mesh=mesh,
        in_specs=(
            P("inst", "tp", None, None, None),
            P("inst", None),
            P("inst", None),
            P("inst", "tp"),
            P("inst", "tp"),
            P("inst", "tp", None, None),
            P("inst", "tp", None, None),
            P("inst"),
            P("inst"),
            P("inst", "tp"),
            P("inst", "tp"),
            P("tp"),
            P(),
        ),
        out_specs=(P("inst", "tp"), P("inst", None, "tp", None, None, None), P("inst", "tp")),
        check_vma=False,
    )
```

```python
import functools

import jax
import jax.numpy as jnp
from jax import lax
from jax.experimental import pallas as pl
from jax.experimental.pallas import tpu as pltpu
from jax.sharding import PartitionSpec as P

MESH = pl.DeviceIdType.MESH
D = 8192
LANES = 128
GROUP = 4
PAGES = 8
FIRST, SECOND = 1, 4
PARTS = 1
STEPS = ((1, 8, 9), (2, 4, 6))


def flipped(index, mask):
    bit = 1
    total = index
    while bit <= mask:
        if mask & bit:
            total = total + bit - 2 * bit * ((index // bit) % 2)
        bit *= 2
    return total


def greets_first(tp, bits):
    top = 1 << (bits.bit_length() - 1)
    side = tp // top % 2
    return side if bits == 1 else 1 - side


def attend(pool, page_of, query, new_kv, length):
    page = pool.shape[2]
    places = [page_of(j) for j in range(PAGES)]
    new_key = new_kv[0:1].astype(jnp.float32)
    new_value = new_kv[1:2].astype(jnp.float32)
    scale = LANES ** (-0.5)
    new_score = jnp.sum(query.astype(jnp.float32) * new_key, axis=1, keepdims=True) * scale
    column = lax.broadcasted_iota(jnp.int32, (query.shape[0], page), 1)
    scores = []
    for j, place in enumerate(places):
        score = lax.dot_general(
            query, pool[place, 0], (((1,), (1,)), ((), ())), preferred_element_type=jnp.float32
        )
        score = score * scale
        position = column + j * page
        score = jnp.where(position == length - 1, new_score, score)
        scores.append(jnp.where(position < length, score, -1e30))
    highest = functools.reduce(jnp.maximum, scores)
    highest = jnp.max(highest, axis=1, keepdims=True)
    weights = [jnp.exp(s - highest) for s in scores]
    share = 1.0 / jnp.sum(functools.reduce(jnp.add, weights), axis=1, keepdims=True)
    mixed = jnp.zeros((query.shape[0], LANES), jnp.float32)
    last = jnp.zeros((query.shape[0], page), jnp.float32)
    for j, (w, place) in enumerate(zip(weights, places)):
        w = (w * share).astype(jnp.bfloat16).astype(jnp.float32)
        is_last = column + j * page == length - 1
        last = last + jnp.where(is_last, w, 0.0)
        w = jnp.where(is_last, 0.0, w).astype(jnp.bfloat16)
        mixed = mixed + jnp.dot(w, pool[place, 1], preferred_element_type=jnp.float32)
    return mixed + jnp.sum(last, axis=1, keepdims=True) * new_value


def kernel(
    mask,
    kv_hbm,
    block_table_hbm,
    mig_table_hbm,
    len_stay_hbm,
    len_mig_hbm,
    query_stay_hbm,
    query_mig_hbm,
    new_stay_hbm,
    new_mig_hbm,
    hidden_stay_hbm,
    hidden_mig_hbm,
    gain_hbm,
    attended,
    arrived,
    normed,
    pool,
    block_table,
    mig_table,
    len_stay,
    len_mig,
    query_stay,
    query_mig,
    new_lines,
    hidden_stay,
    hidden_mig,
    gain,
    out_pages,
    queries,
    mixed,
    rows,
    sums_out,
    sums_in,
    note_out,
    note_in,
    pool_sem,
    load_sem,
    page_send,
    page_recv,
    pass_send,
    pass_recv,
    sum_send,
    sum_recv,
    note_send,
    note_recv,
    answer_sem,
):
    inst, tp = lax.axis_index("inst"), lax.axis_index("tp")
    core = tp % 2
    other = flipped(tp, 1)
    partner = flipped(inst, mask)
    stay = query_stay.shape[0]
    page_count, _, page, _ = pool.shape
    half = out_pages.shape[0]

    part = page_count // PARTS
    pool_loads = [
        pltpu.make_async_copy(
            kv_hbm.at[pl.ds(c * part, part), 0], pool.at[pl.ds(c * part, part)], pool_sem.at[c]
        )
        for c in range(PARTS)
    ]
    pairs = [
        (hidden_stay_hbm, hidden_stay),
        (hidden_mig_hbm, hidden_mig),
        (mig_table_hbm, mig_table),
        (len_mig_hbm, len_mig),
        (new_mig_hbm.at[:, 0], new_lines.at[pl.ds(stay, 1)]),
        (query_stay_hbm, query_stay),
        (query_mig_hbm, query_mig),
        (block_table_hbm, block_table),
        (len_stay_hbm, len_stay),
        (new_stay_hbm.at[:, 0], new_lines.at[pl.ds(0, stay)]),
        (gain_hbm, gain),
    ]
    small_loads = [
        pltpu.make_async_copy(src, dst, load_sem.at[c]) for c, (src, dst) in enumerate(pairs)
    ]
    for load in pool_loads + small_loads[:5]:
        load.start()

    barrier = pltpu.get_barrier_semaphore()
    pl.semaphore_signal(barrier, inc=1, device_id=(partner, tp), device_id_type=MESH)
    steps = STEPS[::-1] if mask in (17, 19) else STEPS
    others = steps[0] + steps[1]
    far = mask % 16 >= 4 or mask in (2, 3)
    answers = 0
    for bits in others:
        first = greets_first(tp, bits) if far else 1
        answers = answers + first

        @pl.when(first == 1)
        def _(bits=bits):
            pl.semaphore_signal(
                barrier, inc=1, device_id=(inst, flipped(tp, bits)), device_id_type=MESH
            )

    for load in small_loads[5:]:
        load.start()

    rows[...] = jnp.zeros_like(rows)
    for load in small_loads[:2]:
        load.wait()
    rows[0:stay, :] = hidden_stay[...].astype(jnp.float32)
    rows[stay : stay + 1, :] = hidden_mig[...].astype(jnp.float32)
    square = rows[...] * rows[...]
    width = square.shape[1]
    sums_out[0] = sum(square[:, c : c + LANES] for c in range(0, width, LANES))

    def sum_copies(step):
        return [
            pltpu.make_async_remote_copy(
                src_ref=sums_out.at[step],
                dst_ref=sums_in.at[step, c],
                send_sem=sum_send.at[step, c],
                recv_sem=sum_recv.at[step, c],
                device_id=(inst, flipped(tp, bits)),
                device_id_type=MESH,
            )
            for c, bits in enumerate(steps[step])
        ]

    def summed(step):
        copies = sum_copies(step)
        for copy in copies:
            copy.wait()
        return sums_out[step] + sum(sums_in[step, c] for c in range(len(copies)))

    def page_copy(j):
        return pltpu.make_async_remote_copy(
            src_ref=out_pages.at[j],
            dst_ref=arrived.at[0, core * half + j, 0],
            send_sem=page_send.at[j],
            recv_sem=page_recv.at[j],
            device_id=(partner, tp),
            device_id_type=MESH,
        )

    def start_sums(step):
        for copy in sum_copies(step):
            copy.start()

    if far:
        pl.semaphore_wait(barrier, 1 + len(others) - answers)
        for bits in others:

            @pl.when(greets_first(tp, bits) == 0)
            def _(bits=bits):
                pl.semaphore_signal(
                    answer_sem, inc=1, device_id=(inst, flipped(tp, bits)), device_id_type=MESH
                )

    else:
        pl.semaphore_wait(barrier, 1 + len(others))
        start_sums(0)

    for load in small_loads[2:5] + pool_loads:
        load.wait()
    length = len_mig[0]
    new_line = new_lines[stay]
    position = lax.broadcasted_iota(jnp.int32, (page, LANES), 0)

    def send_page(j, _):
        at = mig_table[0, core * half + j]
        here = position == length - 1 - (core * half + j) * page
        for k in range(2):
            out_pages[j, k] = jnp.where(here, new_line[k : k + 1], pool[at, k])
        page_copy(j).start()
        return 0

    held = half * (inst // 4 % 2) if mask // 4 % 4 == 2 else 0
    lax.fori_loop(0, half - held, send_page, 0)
    if far:

        @pl.when(answers > 0)
        def _():
            pl.semaphore_wait(answer_sem, answers)

        start_sums(0)

    for load in small_loads[5:]:
        load.wait()
    queries[...] = jnp.zeros_like(queries)
    stay_q, mig_q = query_stay[...].astype(jnp.float32), query_mig[...].astype(jnp.float32)
    for h in range(GROUP):
        queries[0:stay, h, :] = stay_q[:, h * LANES : (h + 1) * LANES]
        queries[stay, h : h + 1, :] = mig_q[:, h * LANES : (h + 1) * LANES]

    own = stay
    note = pltpu.make_async_remote_copy(
        src_ref=note_out,
        dst_ref=note_in,
        send_sem=note_send,
        recv_sem=note_recv,
        device_id=(partner, tp),
        device_id_type=MESH,
    )

    def attend_next(i, _):
        r = own - i
        staying = jnp.minimum(r, stay - 1)

        def page_of(j):
            return jnp.where(r == own, mig_table[0, j], block_table[staying, j])

        mixed[r] = attend(
            pool,
            page_of,
            queries[r].astype(jnp.bfloat16),
            new_lines[r],
            jnp.where(r == own, length, len_stay[staying]),
        )

        @pl.when(i == 0)
        def _():
            if mask // 4 % 4 == 2:
                lax.fori_loop(half - held, half, send_page, 0)

        @pl.when(i == FIRST)
        def _():
            sums_out[1] = summed(0)
            start_sums(1)

        @pl.when(i == SECOND)
        def _():
            sums = summed(1)
            mean_square = jnp.sum(sums, axis=1, keepdims=True) / D
            scaled = rows[...] * lax.rsqrt(mean_square + 1e-05)
            rows[...] = scaled * gain[...].astype(jnp.float32)[None, :]
            line = rows[own : own + 1, :]
            lines = [line[:, h * LANES : (h + 1) * LANES] for h in range(GROUP)]
            note_out[0:8, :] = mixed[own].astype(jnp.bfloat16)
            note_out[8:16, :] = jnp.concatenate(lines + lines, axis=0).astype(jnp.bfloat16)
            note.start()

        return 0

    lax.fori_loop(0, stay + 1, attend_next, 0)

    def pass_copy(j):
        return pltpu.make_async_remote_copy(
            src_ref=arrived.at[0, core * half + j, 0],
            dst_ref=arrived.at[0, core * half + j, 0],
            send_sem=pass_send.at[j],
            recv_sem=pass_recv.at[j],
            device_id=(inst, other),
            device_id_type=MESH,
        )

    def pass_on(j, _):
        page_copy(j).wait_recv()
        pass_copy(j).start()
        return 0

    lax.fori_loop(0, half, pass_on, 0)

    note.wait()
    got = note_in[...].astype(jnp.float32)
    mixed[stay] = got[0:8]
    for h in range(GROUP):
        attended[:, h * LANES : (h + 1) * LANES] = mixed[:, h, :].astype(jnp.bfloat16)
        rows[stay : stay + 1, h * LANES : (h + 1) * LANES] = got[8 + h : 9 + h]
    normed[...] = rows[0 : stay + 1, :].astype(jnp.bfloat16)

    def finish(j, _):
        page_copy(j).wait_send()
        pass_copy(j).wait()
        return 0

    lax.fori_loop(0, half, finish, 0)


def settle(*refs):
    count = (len(refs) - 1) // 2
    copies = [
        pltpu.make_async_copy(refs[c], refs[count + c], refs[-1].at[c]) for c in range(count)
    ]
    for copy in copies:
        copy.start()
    for copy in copies:
        copy.wait()


def local(
    kv_pool,
    block_table,
    mig_table,
    query_stay,
    query_mig,
    new_stay,
    new_mig,
    len_stay,
    len_mig,
    hidden_stay,
    hidden_mig,
    norm_gain,
    partner_mask,
):
    page_count, _, _, page, head = kv_pool.shape
    stay, width = query_stay.shape
    slots = mig_table.shape[1]
    half = slots // 2
    bf16, f32 = jnp.bfloat16, jnp.float32
    vmem = pl.BlockSpec(memory_space=pltpu.VMEM)
    anywhere = pl.BlockSpec(memory_space=pl.ANY)
    dma = pltpu.SemaphoreType.DMA

    operands = (
        kv_pool,
        block_table,
        mig_table,
        len_stay,
        len_mig,
        query_stay,
        query_mig,
        new_stay,
        new_mig,
        hidden_stay,
        hidden_mig,
        norm_gain,
    )
    results = (
        jax.ShapeDtypeStruct((stay + 1, width), bf16),
        jax.ShapeDtypeStruct((1, slots, 1, 2, page, head), bf16),
        jax.ShapeDtypeStruct((stay + 1, width), bf16),
    )

    def matched(mask):
        return pl.pallas_call(
            functools.partial(kernel, mask),
            out_shape=results,
            in_specs=[anywhere] * len(operands),
            out_specs=(vmem, vmem, vmem),
            scratch_shapes=[
                pltpu.VMEM((page_count, 2, page, head), bf16),
                *(pltpu.SMEM(a.shape, a.dtype) for a in operands[1:5]),
                *(pltpu.VMEM(a.shape, a.dtype) for a in operands[5:7]),
                pltpu.VMEM((stay + 1, 2, head), bf16),
                *(pltpu.VMEM(a.shape, a.dtype) for a in operands[9:]),
                pltpu.VMEM((half, 2, page, head), bf16),
                pltpu.VMEM((stay + 1, 8, head), f32),
                pltpu.VMEM((stay + 1, 8, head), f32),
                pltpu.VMEM((8, width), f32),
                pltpu.VMEM((2, 8, LANES), f32),
                pltpu.VMEM((2, 3, 8, LANES), f32),
                pltpu.VMEM((16, LANES), bf16),
                pltpu.VMEM((16, LANES), bf16),
                dma((PARTS,)),
                dma((len(operands) - 1,)),
                dma((half,)),
                dma((half,)),
                dma((half,)),
                dma((half,)),
                dma((2, 3)),
                dma((2, 3)),
                dma,
                dma,
                pltpu.SemaphoreType.REGULAR,
            ],
            compiler_params=pltpu.CompilerParams(
                collective_id=mask - 1, has_side_effects=True, vmem_limit_bytes=32 * 1024 * 1024
            ),
            name="matched",
        )

    branches = [
        lambda *args, mask=mask: tuple(matched(mask)(*args))
        for mask in range(1, lax.axis_size("inst"))
    ]
    found = lax.switch(partner_mask[0] - 1, branches, *operands)
    return pl.pallas_call(
        settle,
        out_shape=results,
        in_specs=[vmem] * 3,
        out_specs=(anywhere,) * 3,
        scratch_shapes=[dma((3,))],
        compiler_params=pltpu.CompilerParams(vmem_limit_bytes=4 * 1024 * 1024),
        name="settle",
    )(*found)


def solution(mesh):
    return jax.shard_map(
        local,
        mesh=mesh,
        in_specs=(
            P("inst", "tp", None, None, None),
            P("inst", None),
            P("inst", None),
            P("inst", "tp"),
            P("inst", "tp"),
            P("inst", "tp", None, None),
            P("inst", "tp", None, None),
            P("inst"),
            P("inst"),
            P("inst", "tp"),
            P("inst", "tp"),
            P("tp"),
            P(),
        ),
        out_specs=(P("inst", "tp"), P("inst", None, "tp", None, None, None), P("inst", "tp")),
        check_vma=False,
    )
```
